32 devices in a mesh: gx: 4 (over y, x), gy: 8 (over z, core).
Axes of the slice: x: 2, y: 2, z: 4, core: 2. Of those that a mesh axis runs over, the one named last changes fastest.
Arguments:
- hidden: bfloat16 [4096, 5376], P('gy', 'gx'), may hold values from -6 to 6
- start: int32 [1], replicated, may hold values from 1024 to 8191
- w_query: bfloat16 [5376, 4096], P('gx', 'gy'), may hold values from -0.078125 to 0.078125
- w_key_value: bfloat16 [5376, 2, 2048], P('gx', None, 'gy'), may hold values from -0.078125 to 0.078125
- w_out: bfloat16 [4096, 5376], P('gy', 'gx'), may hold values from -4 to 4
- cache: bfloat16 [1024, 2, 2048], P(None, None, 'gy'), may hold values from -6 to 6
Outputs:
- attn_branch: bfloat16 [4096, 5376], P('gy', 'gx')
The draws below stay inside these ranges and needn't reach their ends.
All inputs are finite; a program needn't handle non-finite values.
Results may differ from the reference program's by a relative error of at most 0.035.
Values may be sent and summed in bfloat16 or wider, within the bound.
A program may use at most 192 MiB of HBM per device.

```python
import jax
import jax.numpy as jnp
from jax import lax

D = 5376
H = 32
KVH = 16
HD = 128
WINDOW = 1024
BLOCK = 1024
TOKENS = 4096
N_GX = 4
N_GY = 8


def shard_levels(stream_key, extent, cuts, least, high):
    def one(position, blocks):
        heights = jax.random.uniform(jax.random.fold_in(jax.random.fold_in(stream_key, 6), position), (blocks,), jnp.float32, least / len(cuts), high / len(cuts))
        return jnp.repeat(jnp.exp(heights), extent[position] // blocks).reshape((-1,) + (1,) * (len(extent) - position - 1))

    level = one(*cuts[0])
    for cut in cuts[1:]:
        level = level * one(*cut)
    return level


def scatter_about(key, shape, scale, bound, split=(), kind=jnp.bfloat16):
    values = jax.random.normal(key, shape, jnp.float32) * scale
    if len(split) > 0:
        values = shard_levels(key, shape, split, -0.22, 0.18) * values
    return jnp.clip(values, min=-bound, max=bound).astype(kind)


def setup_inputs(seed: int = 0) -> dict:
    seeds = jax.random.split(jax.random.key(seed), 7)
    return {
        "hidden": scatter_about(seeds[0], (TOKENS, D), 1.0, 6.0, ((0, 8), (1, 4))),
        "start": jax.random.randint(seeds[1], (1,), WINDOW, 8192).astype(jnp.int32),
        "w_query": scatter_about(seeds[2], (D, H * HD), D ** -0.5, 0.078125, ((0, 4), (1, 8))),
        "w_key_value": scatter_about(seeds[3], (D, 2, KVH * HD), D ** -0.5, 0.078125, ((0, 4), (2, 8))),
        "w_out": scatter_about(seeds[4], (H * HD, D), 0.3, 4.0, ((0, 8), (1, 4))),
        "cache": scatter_about(seeds[5], (WINDOW, 2, KVH * HD), 1.0, 6.0, ((2, 8),)),
    }


query_scale = 168.0 ** (-0.5)
norm_eps = 1e-06

def unit_rms(values):
    return values * lax.rsqrt(lax.optimization_barrier(jnp.mean(values * values, axis=-1, keepdims=True)) + norm_eps)

def rotate(values, positions):
    head_size = values.shape[-1]
    half_size = head_size // 2
    frequency = 10000.0 ** (-(2.0 * jnp.arange(half_size, dtype=jnp.float32)) / head_size)
    angles = positions.astype(jnp.float32)[:, None] * frequency[None, :]
    cosine = jnp.cos(angles)[:, None, :]
    sine_part = jnp.sin(angles)[:, None, :]
    first_half = values[..., :half_size]
    second = values[..., half_size:]
    return jnp.concatenate([first_half * cosine - second * sine_part, second * cosine + first_half * sine_part], axis=-1)

def attend(queries, query_pos, key_vals, key_pos):
    queries, key_vals = lax.optimization_barrier((queries, key_vals))
    query_wide = queries.astype(jnp.float32)
    kv_wide = key_vals.astype(jnp.float32)
    scores = jnp.einsum('qkgd,skd->qkgs', query_wide, kv_wide[:, 0])
    position_gap = query_pos[:, None] - key_pos[None, :]
    inside = (position_gap >= 0) & (position_gap < WINDOW)
    weights = jnp.where(inside[:, None, None, :], jnp.exp(scores), 0.0)
    denominator = lax.optimization_barrier(jnp.sum(weights, axis=-1))
    rounded = lax.optimization_barrier(weights.astype(jnp.bfloat16))
    summed = jnp.einsum('qkgs,skd->qkgd', rounded.astype(jnp.float32), kv_wide[:, 1])
    return (summed, denominator)

def reference(hidden, start, w_query, w_key_value, w_out, cache):
    slice_width = D // N_GX
    group_size = H // KVH
    columns = jnp.concatenate([w_query, w_key_value.reshape(D, 2 * KVH * HD)], axis=1)
    total_cols = columns.shape[1]
    hidden_parts = hidden.reshape(TOKENS, N_GX, slice_width)
    column_parts = columns.reshape(N_GX, slice_width, total_cols)

    def add_slice(running_sum, part_index):
        partial_value = jnp.dot(hidden_parts[:, part_index, :], column_parts[part_index], preferred_element_type=jnp.float32)
        rounded = lax.optimization_barrier(partial_value.astype(jnp.bfloat16))
        return (running_sum + rounded.astype(jnp.float32), None)
    summed_cols, unused = lax.scan(add_slice, jnp.zeros((TOKENS, total_cols), jnp.float32), jnp.arange(N_GX, dtype=jnp.int32))
    projected = summed_cols.astype(jnp.bfloat16)
    positions = start[0] + jnp.arange(TOKENS, dtype=jnp.int32)
    query_heads = projected[:, :H * HD].reshape(TOKENS, H, HD).astype(jnp.float32)
    queries = (rotate(unit_rms(query_heads), positions) * query_scale).astype(jnp.bfloat16)
    queries = queries.reshape(TOKENS, KVH, group_size, HD)
    kv_pairs = projected[:, H * HD:].reshape(TOKENS, 2, KVH, HD)
    key_part = rotate(unit_rms(kv_pairs[:, 0].astype(jnp.float32)), positions).astype(jnp.bfloat16)
    new_kv = jnp.stack([key_part, kv_pairs[:, 1]], axis=1)
    joined = jnp.concatenate([cache.reshape(WINDOW, 2, KVH, HD), new_kv], axis=0)
    joined_pos = start[0] - WINDOW + jnp.arange(WINDOW + TOKENS, dtype=jnp.int32)

    def one_block(block_index):
        row_start = (block_index * BLOCK).astype(jnp.int32)
        query_block = lax.dynamic_slice_in_dim(queries, row_start, BLOCK, 0)
        query_pos = lax.dynamic_slice_in_dim(positions, row_start, BLOCK, 0)
        context = lax.dynamic_slice_in_dim(joined, row_start, WINDOW + BLOCK, 0)
        context_pos = lax.dynamic_slice_in_dim(joined_pos, row_start, WINDOW + BLOCK, 0)
        summed, denominator = attend(query_block, query_pos, context, context_pos)
        return (summed / denominator[..., None]).reshape(BLOCK, H * HD).astype(jnp.bfloat16)
    mixed = lax.map(one_block, jnp.arange(N_GX, dtype=jnp.int32)).reshape(TOKENS, H * HD)
    group_cols = H // N_GY * HD
    mixed_parts = mixed.reshape(TOKENS, N_GY, group_cols)
    out_parts = w_out.reshape(N_GY, group_cols, D)

    def add_group(running_sum, part_index):
        partial_value = jnp.dot(mixed_parts[:, part_index, :], out_parts[part_index], preferred_element_type=jnp.float32)
        rounded = lax.optimization_barrier(partial_value.astype(jnp.bfloat16))
        return (running_sum + rounded.astype(jnp.float32), None)
    out_sum, unused = lax.scan(add_group, jnp.zeros((TOKENS, D), jnp.float32), jnp.arange(N_GY, dtype=jnp.int32))
    return out_sum.astype(jnp.bfloat16)
```

```python
import jax
import jax.numpy as jnp
from jax import lax
from jax.experimental import pallas as pl
from jax.experimental.pallas import tpu as pltpu
from jax.sharding import PartitionSpec as P

HD = 128
WINDOW = 1024


query_scale = 168.0 ** (-0.5)
norm_eps = 1e-06


def shifted_2(value, axis, by):
    length = lax.axis_size(axis)
    pairs = [(i, i + by) for i in range(length) if 0 <= i + by < length]
    return lax.ppermute(value, axis, pairs)


def unit_rms(values):
    return values * lax.rsqrt(jnp.mean(values * values, axis=-1, keepdims=True) + norm_eps)


def rotate(values, positions):
    head_size = values.shape[-1]
    half_size = head_size // 2
    frequency = 10000.0 ** (-(2.0 * jnp.arange(half_size, dtype=jnp.float32)) / head_size)
    angles = positions.astype(jnp.float32)[:, None] * frequency[None, :]
    cosine = jnp.cos(angles)[:, None, :]
    sine_part = jnp.sin(angles)[:, None, :]
    first_half = values[..., :half_size]
    second = values[..., half_size:]
    return jnp.concatenate(
        [first_half * cosine - second * sine_part, second * cosine + first_half * sine_part],
        axis=-1,
    )


def attend(queries, query_pos, key_vals, key_pos):
    scores = jnp.einsum(
        "qkgd,skd->qkgs", queries, key_vals[:, 0], preferred_element_type=jnp.float32
    )
    position_gap = query_pos[:, None] - key_pos[None, :]
    inside = (position_gap >= 0) & (position_gap < WINDOW)
    weights = jnp.where(inside[:, None, None, :], jnp.exp(scores), 0.0)
    denominator = jnp.sum(weights, axis=-1)
    summed = jnp.einsum(
        "qkgs,skd->qkgd",
        weights.astype(jnp.bfloat16),
        key_vals[:, 1],
        preferred_element_type=jnp.float32,
    )
    return (summed, denominator)


def plain_shards(hidden, start, w_query, w_key_value, w_out, cache):
    model_slice = hidden.shape[1]
    query_cols = w_query.shape[1]
    kv_heads = w_key_value.shape[2] // HD
    query_heads = query_cols // HD
    group_size = query_heads // kv_heads
    gx_count = lax.axis_size("gx")
    gx_index = lax.axis_index("gx")
    first_pos = start[0]
    rows_all = lax.all_gather(hidden, "gy", axis=0, tiled=True)
    token_count = rows_all.shape[0]
    block_rows = token_count // gx_count
    kv_weight = w_key_value.reshape(model_slice, 2 * kv_heads * HD)
    cache_kv = cache.reshape(WINDOW, 2, kv_heads, HD)
    query_pos = first_pos + gx_index * block_rows + jnp.arange(block_rows, dtype=jnp.int32)
    united_weight = jnp.concatenate([w_query, kv_weight], axis=1)
    row_slice = rows_all
    projected = lax.psum_scatter(
        jnp.dot(row_slice, united_weight, preferred_element_type=jnp.float32).astype(jnp.bfloat16),
        "gx",
        scatter_dimension=0,
        tiled=True,
    )
    heads_wide = projected[:, :query_cols].reshape(block_rows, query_heads, HD).astype(jnp.float32)
    rotated = (rotate(unit_rms(heads_wide), query_pos) * query_scale).astype(jnp.bfloat16)
    queries = rotated.reshape(block_rows, kv_heads, group_size, HD)
    kv_rows = projected[:, query_cols:]
    row_count = kv_rows.shape[0]
    kv_pairs = kv_rows.reshape(row_count, 2, kv_heads, HD)
    key_part = rotate(unit_rms(kv_pairs[:, 0].astype(jnp.float32)), query_pos).astype(jnp.bfloat16)
    own_kv = jnp.stack([key_part, kv_pairs[:, 1]], axis=1)
    reach_blocks = WINDOW // block_rows
    key_pieces = [own_kv]
    shifted = shifted_2(own_kv, "gx", 1)
    key_pieces.insert(0, jnp.where(gx_index >= 1, shifted, cache_kv))
    context = jnp.concatenate(key_pieces, axis=0)
    context_pos = (
        first_pos
        + (gx_index - reach_blocks) * block_rows
        + jnp.arange((reach_blocks + 1) * block_rows, dtype=jnp.int32)
    )
    summed, denominator = attend(queries, query_pos, context, context_pos)
    mixed_heads = (
        (summed / denominator[..., None]).reshape(block_rows, query_cols).astype(jnp.bfloat16)
    )
    head_rows = lax.all_gather(mixed_heads, "gx", axis=0, tiled=True)
    row_slice = head_rows
    return lax.psum_scatter(
        jnp.dot(row_slice, w_out, preferred_element_type=jnp.float32).astype(jnp.bfloat16),
        "gy",
        scatter_dimension=0,
        tiled=True,
    )


def planes_orders(planes):
    arrive, depart = [], []
    for z in range(planes):
        found = [(0, 0, z)]
        for hop in range(1, planes):
            if z - hop >= 0:
                found.append((1, hop, z - hop))
            if z + hop < planes:
                found.append((-1, hop, z + hop))
        arrive.append(found)
        far = sorted((d for d in range(planes) if d != z), key=lambda d: -abs(d - z))
        if len(far) > 1 and abs(far[-1] - z) == abs(far[-2] - z):
            right = z + 1 if z >= planes // 2 else z - 1
            far = [right] + [d for d in far if d != right]
        depart.append(far + [z])
    return arrive, depart


def pick(z, choices):
    value = choices[0]
    for place in range(1, len(choices)):
        if choices[place] is not choices[place - 1]:
            value = jnp.where(z >= place, choices[place], value)
    return value


def prepare_kernel(own_ref, x_ref, y_ref, d_ref, cos_ref, sin_ref, q_ref, kv_ref):
    total = own_ref[...].astype(jnp.float32) + x_ref[...].astype(jnp.float32)
    total = total + y_ref[...].astype(jnp.float32) + d_ref[...].astype(jnp.float32)
    total = total.astype(jnp.bfloat16)
    cosine, sine = cos_ref[...], sin_ref[...]

    def turned(columns, scale):
        wide = columns.astype(jnp.float32)
        wide = wide * lax.rsqrt(jnp.mean(wide * wide, axis=-1, keepdims=True) + norm_eps)
        return ((wide * cosine + pltpu.roll(wide, HD // 2, 1) * sine) * scale).astype(jnp.bfloat16)

    q_ref[:, :HD] = turned(total[:, :HD], query_scale)
    q_ref[:, HD : 2 * HD] = turned(total[:, HD : 2 * HD], query_scale)
    kv_ref[:, :HD] = turned(total[:, 2 * HD : 3 * HD], 1.0)
    kv_ref[:, HD:] = total[:, 3 * HD :]


def attend_kernel(index_ref, q_ref, old_ref, mid_ref, now_ref, out_ref):
    del index_ref
    rows = q_ref.shape[1]
    tile = rows // 2
    for head in range(2):
        for part in range(2):
            query = q_ref[0, part * tile : (part + 1) * tile, head * HD : (head + 1) * HD]
            row = lax.broadcasted_iota(jnp.int32, (tile, tile), 0)
            col = lax.broadcasted_iota(jnp.int32, (tile, tile), 1)
            pieces = [(mid_ref, 0, rows, 0), (old_ref, part * tile, tile, 1), (now_ref, part * tile, tile, -1)]
            if part == 0:
                pieces.append((old_ref, tile, tile, 0))
            else:
                pieces.append((now_ref, 0, tile, 0))
            total = jnp.zeros((tile, HD), jnp.float32)
            weight_sum = jnp.zeros((tile, 1), jnp.float32)
            for ref, first, count, mask in pieces:
                key = ref[0, first : first + count, :HD]
                value = ref[0, first : first + count, HD:]
                scores = lax.dot_general(
                    query, key, (((1,), (1,)), ((), ())), preferred_element_type=jnp.float32
                )
                weights = jnp.exp(scores)
                if mask == 1:
                    weights = jnp.where(col > row, weights, 0.0)
                elif mask == -1:
                    weights = jnp.where(col <= row, weights, 0.0)
                weight_sum += jnp.sum(weights, axis=-1, keepdims=True)
                total += jnp.dot(
                    weights.astype(jnp.bfloat16), value, preferred_element_type=jnp.float32
                )
            out_ref[part * tile : (part + 1) * tile, head * HD : (head + 1) * HD] = (
                total / weight_sum
            ).astype(jnp.bfloat16)


def line_shards(hidden, start, w_query, w_key_value, w_out, cache):
    rows, width = hidden.shape
    gy_count = lax.axis_size("gy")
    gx_count = lax.axis_size("gx")
    planes = gy_count // 2
    gy_index = lax.axis_index("gy")
    gx_index = lax.axis_index("gx")
    z, core = gy_index // 2, gy_index % 2
    y, x = gx_index // 2, gx_index % 2
    arrive, depart = planes_orders(planes)

    def over_gx(value, flip):
        return lax.ppermute(value, "gx", [(i, i ^ flip) for i in range(gx_count)])

    def over_core(value):
        return lax.ppermute(value, "gy", [(i, i ^ 1) for i in range(gy_count)])

    def along(value, by, senders):
        pairs = [(2 * s + c, 2 * (s + by) + c) for s in senders for c in range(2)]
        return lax.ppermute(value, "gy", pairs)

    moved = {(0, 0): hidden}
    for hop in range(1, planes):
        for way in (1, -1):
            before = hidden if hop == 1 else moved[(way, hop - 1)]
            senders = [
                s
                for s in range(planes)
                if 0 <= s + way < planes and 0 <= s - way * (hop - 1) < planes
            ]
            moved[(way, hop)] = along(before, way, senders)

    kv = w_key_value.reshape(width, 2, 2, HD)
    own_w = jnp.stack(
        [
            jnp.concatenate([w_query[:, g * 2 * HD : (g + 1) * 2 * HD], kv[:, 0, g], kv[:, 1, g]], axis=1)
            for g in range(2)
        ]
    )
    other_w = over_core(own_w)
    same = core == y
    near_w = jnp.where(same, own_w, other_w)
    far_w = jnp.where(same, other_w, own_w)
    w_self = jnp.where(x == 0, near_w[0], near_w[1])
    w_x = jnp.where(x == 0, near_w[1], near_w[0])
    w_y = jnp.where(x == 0, far_w[0], far_w[1])
    w_d = jnp.where(x == 0, far_w[1], far_w[0])

    own_o = w_out.reshape(2, 2 * HD, -1)
    other_o = over_core(own_o)
    near_o = jnp.where(same, own_o, other_o)
    far_o = jnp.where(same, other_o, own_o)
    o_all = jnp.concatenate(
        [
            jnp.where(x == 0, near_o[0], near_o[1]),
            jnp.where(x == 0, near_o[1], near_o[0]),
            jnp.where(x == 0, far_o[0], far_o[1]),
            jnp.where(x == 0, far_o[1], far_o[0]),
        ],
        axis=0,
    )

    cache_heads = cache.reshape(2, rows, 2, 2, HD)
    mine = jnp.where(x == 0, cache_heads[:, :, :, 0], cache_heads[:, :, :, 1]).reshape(2, rows, 2 * HD)
    mine = jnp.where(same, mine, over_core(mine))
    cache_own = jnp.where(core == 0, mine[0], mine[1])
    cache_other = jnp.where(core == 0, mine[1], mine[0])

    chunk_at = jnp.asarray([[c for _, _, c in a] for a in arrive], jnp.int32)[z]
    half = HD // 2
    frequency = 10000.0 ** (-(2.0 * jnp.arange(half, dtype=jnp.float32)) / HD)
    places = start[0] + (chunk_at * 2 + core)[:, None] * rows + jnp.arange(rows, dtype=jnp.int32)
    angles = places.astype(jnp.float32)[:, :, None] * frequency
    cosine, sine = jnp.cos(angles), jnp.sin(angles)
    cosine = jnp.concatenate([cosine, cosine], axis=-1)
    sine = jnp.concatenate([-sine, sine], axis=-1)

    prepare = pl.pallas_call(
        prepare_kernel,
        out_shape=[jax.ShapeDtypeStruct((rows, 2 * HD), jnp.bfloat16)] * 2,
        in_specs=[pl.BlockSpec(memory_space=pltpu.VMEM)] * 6,
        out_specs=[pl.BlockSpec(memory_space=pltpu.VMEM)] * 2,
        cost_estimate=pl.CostEstimate(flops=rows * 8192, bytes_accessed=rows * 6144, transcendentals=0),
        compiler_params=pltpu.CompilerParams(vmem_limit_bytes=24 * 2**20),
    )
    queries, kv_own, kv_other = [], [cache_own], [cache_other]
    for step in range(planes):
        block = pick(z, [moved[arrive[p][step][:2]] for p in range(planes)])

        def product(weight):
            return jnp.dot(block, weight, preferred_element_type=jnp.float32).astype(jnp.bfloat16)

        from_d = over_gx(product(w_d), 3)
        from_x = over_gx(product(w_x), 1)
        from_y = over_gx(product(w_y), 2)
        query, pair = prepare(product(w_self), from_x, from_y, from_d, cosine[step], sine[step])
        queries.append(query)
        kv_own.append(pair)
        kv_other.append(over_core(pair))
    queries = jnp.stack(queries)
    kv_own = jnp.stack(kv_own)
    kv_other = jnp.stack(kv_other)

    table = []
    for p in range(planes):
        step_of = {c: s for s, (_, _, c) in enumerate(arrive[p])}
        at = lambda c: 0 if c < 0 else 1 + step_of[c]
        table.append([[[step_of[c], at(c - 1), at(c - 1) if k == 0 else at(c), at(c)] for c in depart[p]] for k in range(2)])
    indices = jnp.asarray(table, jnp.int32)[z, core]

    kv_block = (1, rows, 2 * HD)
    attend_call = pl.pallas_call(
        attend_kernel,
        out_shape=jax.ShapeDtypeStruct((rows, 2 * HD), jnp.bfloat16),
        grid_spec=pltpu.PrefetchScalarGridSpec(
            num_scalar_prefetch=1,
            grid=(1,),
            in_specs=[
                pl.BlockSpec(kv_block, lambda i, t: (t[0], 0, 0)),
                pl.BlockSpec(kv_block, lambda i, t: (t[1], 0, 0)),
                pl.BlockSpec(kv_block, lambda i, t: (t[2], 0, 0)),
                pl.BlockSpec(kv_block, lambda i, t: (t[3], 0, 0)),
            ],
            out_specs=pl.BlockSpec((rows, 2 * HD), lambda i, t: (0, 0)),
        ),
        cost_estimate=pl.CostEstimate(
            flops=8 * rows * 3 * rows * HD, bytes_accessed=rows * 2560, transcendentals=6 * rows * rows
        ),
        compiler_params=pltpu.CompilerParams(vmem_limit_bytes=24 * 2**20),
    )
    parts = []
    for step in range(planes):
        mixed = attend_call(indices[step], queries, kv_own, kv_other, kv_own)
        gathered = jnp.concatenate(
            [mixed, over_gx(mixed, 1), over_gx(mixed, 2), over_gx(mixed, 3)], axis=1
        )
        parts.append(
            jnp.dot(gathered, o_all, preferred_element_type=jnp.float32).astype(jnp.bfloat16)
        )

    arrived = {1: None, -1: None}
    for offset in range(planes - 1, 0, -1):
        for way in (1, -1):
            senders = [s for s in range(planes) if 0 <= s + way * offset < planes]
            steps = {s: depart[s].index(s + way * offset) for s in senders}
            filled = [steps.get(s, steps[min(senders, key=lambda q: abs(q - s))]) for s in range(planes)]
            value = pick(z, [parts[s] for s in filled])
            if arrived[way] is not None:
                value = (value.astype(jnp.float32) + arrived[way].astype(jnp.float32)).astype(jnp.bfloat16)
            arrived[way] = along(value, way, senders)
    total = parts[-1].astype(jnp.float32)
    total = total + arrived[1].astype(jnp.float32) + arrived[-1].astype(jnp.float32)
    return total.astype(jnp.bfloat16)


def shards(hidden, start, w_query, w_key_value, w_out, cache):
    gx_count, gy_count = lax.axis_size("gx"), lax.axis_size("gy")
    fits = (
        gx_count == 4
        and gy_count == 8
        and w_query.shape[1] == 4 * HD
        and w_key_value.shape[2] == 2 * HD
        and 2 * hidden.shape[0] == WINDOW
    )
    run = line_shards if fits else plain_shards
    return run(hidden, start, w_query, w_key_value, w_out, cache)


def solution(mesh):
    return jax.shard_map(
        shards,
        mesh=mesh,
        in_specs=(
            P("gy", "gx"),
            P(),
            P("gx", "gy"),
            P("gx", None, "gy"),
            P("gy", "gx"),
            P(None, None, "gy"),
        ),
        out_specs=P("gy", "gx"),
        check_vma=False,
    )
```

```python
import jax
import jax.numpy as jnp
from jax import lax
from jax.experimental import pallas as pl
from jax.experimental.pallas import tpu as pltpu
from jax.sharding import PartitionSpec as P

HD = 128
WINDOW = 1024


query_scale = 168.0 ** (-0.5)
norm_eps = 1e-06


def shifted_2(value, axis, by):
    length = lax.axis_size(axis)
    pairs = [(i, i + by) for i in range(length) if 0 <= i + by < length]
    return lax.ppermute(value, axis, pairs)


def unit_rms(values):
    return values * lax.rsqrt(jnp.mean(values * values, axis=-1, keepdims=True) + norm_eps)


def rotate(values, positions):
    head_size = values.shape[-1]
    half_size = head_size // 2
    frequency = 10000.0 ** (-(2.0 * jnp.arange(half_size, dtype=jnp.float32)) / head_size)
    angles = positions.astype(jnp.float32)[:, None] * frequency[None, :]
    cosine = jnp.cos(angles)[:, None, :]
    sine_part = jnp.sin(angles)[:, None, :]
    first_half = values[..., :half_size]
    second = values[..., half_size:]
    return jnp.concatenate(
        [first_half * cosine - second * sine_part, second * cosine + first_half * sine_part],
        axis=-1,
    )


def attend(queries, query_pos, key_vals, key_pos):
    scores = jnp.einsum(
        "qkgd,skd->qkgs", queries, key_vals[:, 0], preferred_element_type=jnp.float32
    )
    position_gap = query_pos[:, None] - key_pos[None, :]
    inside = (position_gap >= 0) & (position_gap < WINDOW)
    weights = jnp.where(inside[:, None, None, :], jnp.exp(scores), 0.0)
    denominator = jnp.sum(weights, axis=-1)
    summed = jnp.einsum(
        "qkgs,skd->qkgd",
        weights.astype(jnp.bfloat16),
        key_vals[:, 1],
        preferred_element_type=jnp.float32,
    )
    return (summed, denominator)


def plain_shards(hidden, start, w_query, w_key_value, w_out, cache):
    model_slice = hidden.shape[1]
    query_cols = w_query.shape[1]
    kv_heads = w_key_value.shape[2] // HD
    query_heads = query_cols // HD
    group_size = query_heads // kv_heads
    gx_count = lax.axis_size("gx")
    gx_index = lax.axis_index("gx")
    first_pos = start[0]
    rows_all = lax.all_gather(hidden, "gy", axis=0, tiled=True)
    token_count = rows_all.shape[0]
    block_rows = token_count // gx_count
    kv_weight = w_key_value.reshape(model_slice, 2 * kv_heads * HD)
    cache_kv = cache.reshape(WINDOW, 2, kv_heads, HD)
    query_pos = first_pos + gx_index * block_rows + jnp.arange(block_rows, dtype=jnp.int32)
    united_weight = jnp.concatenate([w_query, kv_weight], axis=1)
    row_slice = rows_all
    projected = lax.psum_scatter(
        jnp.dot(row_slice, united_weight, preferred_element_type=jnp.float32).astype(jnp.bfloat16),
        "gx",
        scatter_dimension=0,
        tiled=True,
    )
    heads_wide = projected[:, :query_cols].reshape(block_rows, query_heads, HD).astype(jnp.float32)
    rotated = (rotate(unit_rms(heads_wide), query_pos) * query_scale).astype(jnp.bfloat16)
    queries = rotated.reshape(block_rows, kv_heads, group_size, HD)
    kv_rows = projected[:, query_cols:]
    row_count = kv_rows.shape[0]
    kv_pairs = kv_rows.reshape(row_count, 2, kv_heads, HD)
    key_part = rotate(unit_rms(kv_pairs[:, 0].astype(jnp.float32)), query_pos).astype(jnp.bfloat16)
    own_kv = jnp.stack([key_part, kv_pairs[:, 1]], axis=1)
    reach_blocks = WINDOW // block_rows
    key_pieces = [own_kv]
    shifted = shifted_2(own_kv, "gx", 1)
    key_pieces.insert(0, jnp.where(gx_index >= 1, shifted, cache_kv))
    context = jnp.concatenate(key_pieces, axis=0)
    context_pos = (
        first_pos
        + (gx_index - reach_blocks) * block_rows
        + jnp.arange((reach_blocks + 1) * block_rows, dtype=jnp.int32)
    )
    summed, denominator = attend(queries, query_pos, context, context_pos)
    mixed_heads = (
        (summed / denominator[..., None]).reshape(block_rows, query_cols).astype(jnp.bfloat16)
    )
    head_rows = lax.all_gather(mixed_heads, "gx", axis=0, tiled=True)
    row_slice = head_rows
    return lax.psum_scatter(
        jnp.dot(row_slice, w_out, preferred_element_type=jnp.float32).astype(jnp.bfloat16),
        "gy",
        scatter_dimension=0,
        tiled=True,
    )


def planes_orders(planes):
    arrive, depart = [], []
    for z in range(planes):
        found = [(0, 0, z)]
        for hop in range(1, planes):
            if z - hop >= 0:
                found.append((1, hop, z - hop))
            if z + hop < planes:
                found.append((-1, hop, z + hop))
        arrive.append(found)
        far = sorted((d for d in range(planes) if d != z), key=lambda d: -abs(d - z))
        if len(far) > 1 and abs(far[-1] - z) == abs(far[-2] - z):
            right = z + 1 if z >= planes // 2 else z - 1
            far = [right] + [d for d in far if d != right]
        depart.append(far + [z])
    return arrive, depart


def pick(z, choices):
    value = choices[0]
    for place in range(1, len(choices)):
        if choices[place] is not choices[place - 1]:
            value = jnp.where(z >= place, choices[place], value)
    return value


def prepare_kernel(own_ref, x_ref, y_ref, d_ref, cos_ref, sin_ref, q_ref, kv_ref):
    total = own_ref[...].astype(jnp.float32) + x_ref[...].astype(jnp.float32)
    total = total + y_ref[...].astype(jnp.float32) + d_ref[...].astype(jnp.float32)
    total = total.astype(jnp.bfloat16)
    cosine, sine = cos_ref[...], sin_ref[...]

    def turned(columns, scale):
        wide = columns.astype(jnp.float32)
        wide = wide * lax.rsqrt(jnp.mean(wide * wide, axis=-1, keepdims=True) + norm_eps)
        return ((wide * cosine + pltpu.roll(wide, HD // 2, 1) * sine) * scale).astype(jnp.bfloat16)

    q_ref[:, :HD] = turned(total[:, :HD], query_scale)
    q_ref[:, HD : 2 * HD] = turned(total[:, HD : 2 * HD], query_scale)
    kv_ref[:, :HD] = turned(total[:, 2 * HD : 3 * HD], 1.0)
    kv_ref[:, HD:] = total[:, 3 * HD :]


def attend_kernel(index_ref, q_ref, old_ref, mid_ref, now_ref, out_ref):
    del index_ref
    rows = q_ref.shape[1]
    tile = rows // 2
    for head in range(2):
        for part in range(2):
            query = q_ref[0, part * tile : (part + 1) * tile, head * HD : (head + 1) * HD]
            row = lax.broadcasted_iota(jnp.int32, (tile, tile), 0)
            col = lax.broadcasted_iota(jnp.int32, (tile, tile), 1)
            pieces = [(mid_ref, 0, rows, 0), (old_ref, part * tile, tile, 1), (now_ref, part * tile, tile, -1)]
            if part == 0:
                pieces.append((old_ref, tile, tile, 0))
            else:
                pieces.append((now_ref, 0, tile, 0))
            total = jnp.zeros((tile, HD), jnp.float32)
            weight_sum = jnp.zeros((tile, 1), jnp.float32)
            for ref, first, count, mask in pieces:
                key = ref[0, first : first + count, :HD]
                value = ref[0, first : first + count, HD:]
                scores = lax.dot_general(
                    query, key, (((1,), (1,)), ((), ())), preferred_element_type=jnp.float32
                )
                weights = jnp.exp(scores)
                if mask == 1:
                    weights = jnp.where(col > row, weights, 0.0)
                elif mask == -1:
                    weights = jnp.where(col <= row, weights, 0.0)
                weight_sum += jnp.sum(weights, axis=-1, keepdims=True)
                total += jnp.dot(
                    weights.astype(jnp.bfloat16), value, preferred_element_type=jnp.float32
                )
            out_ref[part * tile : (part + 1) * tile, head * HD : (head + 1) * HD] = (
                total / weight_sum
            ).astype(jnp.bfloat16)


def line_shards(hidden, start, w_query, w_key_value, w_out, cache):
    rows, width = hidden.shape
    gy_count = lax.axis_size("gy")
    gx_count = lax.axis_size("gx")
    planes = gy_count // 2
    gy_index = lax.axis_index("gy")
    gx_index = lax.axis_index("gx")
    z, core = gy_index // 2, gy_index % 2
    y, x = gx_index // 2, gx_index % 2
    arrive, depart = planes_orders(planes)

    def over_gx(value, flip):
        return lax.ppermute(value, "gx", [(i, i ^ flip) for i in range(gx_count)])

    def over_core(value):
        return lax.ppermute(value, "gy", [(i, i ^ 1) for i in range(gy_count)])

    def along(value, by, senders):
        pairs = [(2 * s + c, 2 * (s + by) + c) for s in senders for c in range(2)]
        return lax.ppermute(value, "gy", pairs)

    moved = {(0, 0): hidden}
    for hop in range(1, planes):
        for way in (1, -1):
            before = hidden if hop == 1 else moved[(way, hop - 1)]
            senders = [
                s
                for s in range(planes)
                if 0 <= s + way < planes and 0 <= s - way * (hop - 1) < planes
            ]
            moved[(way, hop)] = along(before, way, senders)

    kv = w_key_value.reshape(width, 2, 2, HD)
    own_w = jnp.stack(
        [
            jnp.concatenate([w_query[:, g * 2 * HD : (g + 1) * 2 * HD], kv[:, 0, g], kv[:, 1, g]], axis=1)
            for g in range(2)
        ]
    )
    other_w = over_core(own_w)
    same = core == y
    near_w = jnp.where(same, own_w, other_w)
    far_w = jnp.where(same, other_w, own_w)
    w_self = jnp.where(x == 0, near_w[0], near_w[1])
    w_x = jnp.where(x == 0, near_w[1], near_w[0])
    w_y = jnp.where(x == 0, far_w[0], far_w[1])
    w_d = jnp.where(x == 0, far_w[1], far_w[0])

    own_o = w_out.reshape(2, 2 * HD, -1)
    other_o = over_core(own_o)
    near_o = jnp.where(same, own_o, other_o)
    far_o = jnp.where(same, other_o, own_o)
    o_all = jnp.concatenate(
        [
            jnp.where(x == 0, near_o[0], near_o[1]),
            jnp.where(x == 0, near_o[1], near_o[0]),
            jnp.where(x == 0, far_o[0], far_o[1]),
            jnp.where(x == 0, far_o[1], far_o[0]),
        ],
        axis=0,
    )

    cache_heads = cache.reshape(2, rows, 2, 2, HD)
    mine = jnp.where(x == 0, cache_heads[:, :, :, 0], cache_heads[:, :, :, 1]).reshape(2, rows, 2 * HD)
    mine = jnp.where(same, mine, over_core(mine))
    cache_own = jnp.where(core == 0, mine[0], mine[1])
    cache_other = jnp.where(core == 0, mine[1], mine[0])

    chunk_at = jnp.asarray([[c for _, _, c in a] for a in arrive], jnp.int32)[z]
    half = HD // 2
    frequency = 10000.0 ** (-(2.0 * jnp.arange(half, dtype=jnp.float32)) / HD)
    places = start[0] + (chunk_at * 2 + core)[:, None] * rows + jnp.arange(rows, dtype=jnp.int32)
    angles = places.astype(jnp.float32)[:, :, None] * frequency
    cosine, sine = jnp.cos(angles), jnp.sin(angles)
    cosine = jnp.concatenate([cosine, cosine], axis=-1)
    sine = jnp.concatenate([-sine, sine], axis=-1)

    prepare = pl.pallas_call(
        prepare_kernel,
        out_shape=[jax.ShapeDtypeStruct((rows, 2 * HD), jnp.bfloat16)] * 2,
        in_specs=[pl.BlockSpec(memory_space=pltpu.VMEM)] * 6,
        out_specs=[pl.BlockSpec(memory_space=pltpu.VMEM)] * 2,
        cost_estimate=pl.CostEstimate(flops=rows * 8192, bytes_accessed=rows * 6144, transcendentals=0),
        compiler_params=pltpu.CompilerParams(vmem_limit_bytes=24 * 2**20),
    )
    queries, kv_own, kv_other = [], [cache_own], [cache_other]

    def finish(step):
        query, pair = prepare(own, from_x, from_y, from_d, cosine[step], sine[step])
        queries.append(query)
        kv_own.append(pair)
        kv_other.append(over_core(pair))

    for step in range(planes):
        used = sorted({arrive[p][step][:2] for p in range(planes)})
        block = pick(z, [moved[arrive[p][step][:2]] for p in range(planes)])
        if step > 0:
            block, from_x, from_y, from_d, *again = lax.optimization_barrier(
                (block, from_x, from_y, from_d, *[moved[u] for u in used])
            )
            moved.update(zip(used, again))
            finish(step - 1)

        def product(weight):
            return jnp.dot(block, weight, preferred_element_type=jnp.float32).astype(jnp.bfloat16)

        from_d = over_gx(product(w_d), 3)
        from_x = over_gx(product(w_x), 1)
        from_y = over_gx(product(w_y), 2)
        own = product(w_self)
    finish(planes - 1)
    queries = jnp.stack(queries)
    kv_own = jnp.stack(kv_own)
    kv_other = jnp.stack(kv_other)

    table = []
    for p in range(planes):
        step_of = {c: s for s, (_, _, c) in enumerate(arrive[p])}
        at = lambda c: 0 if c < 0 else 1 + step_of[c]
        table.append([[[step_of[c], at(c - 1), at(c - 1) if k == 0 else at(c), at(c)] for c in depart[p]] for k in range(2)])
    indices = jnp.asarray(table, jnp.int32)[z, core]

    kv_block = (1, rows, 2 * HD)
    attend_call = pl.pallas_call(
        attend_kernel,
        out_shape=jax.ShapeDtypeStruct((rows, 2 * HD), jnp.bfloat16),
        grid_spec=pltpu.PrefetchScalarGridSpec(
            num_scalar_prefetch=1,
            grid=(1,),
            in_specs=[
                pl.BlockSpec(kv_block, lambda i, t: (t[0], 0, 0)),
                pl.BlockSpec(kv_block, lambda i, t: (t[1], 0, 0)),
                pl.BlockSpec(kv_block, lambda i, t: (t[2], 0, 0)),
                pl.BlockSpec(kv_block, lambda i, t: (t[3], 0, 0)),
            ],
            out_specs=pl.BlockSpec((rows, 2 * HD), lambda i, t: (0, 0)),
        ),
        cost_estimate=pl.CostEstimate(
            flops=8 * rows * 3 * rows * HD, bytes_accessed=rows * 2560, transcendentals=6 * rows * rows
        ),
        compiler_params=pltpu.CompilerParams(vmem_limit_bytes=24 * 2**20),
    )
    parts = []
    for step in range(planes):
        mixed = attend_call(indices[step], queries, kv_own, kv_other, kv_own)
        gathered = jnp.concatenate(
            [mixed, over_gx(mixed, 1), over_gx(mixed, 2), over_gx(mixed, 3)], axis=1
        )
        parts.append(
            jnp.dot(gathered, o_all, preferred_element_type=jnp.float32).astype(jnp.bfloat16)
        )

    arrived = {1: None, -1: None}
    for offset in range(planes - 1, 0, -1):
        for way in (1, -1):
            senders = [s for s in range(planes) if 0 <= s + way * offset < planes]
            steps = {s: depart[s].index(s + way * offset) for s in senders}
            filled = [steps.get(s, steps[min(senders, key=lambda q: abs(q - s))]) for s in range(planes)]
            value = pick(z, [parts[s] for s in filled])
            if arrived[way] is not None:
                value = (value.astype(jnp.float32) + arrived[way].astype(jnp.float32)).astype(jnp.bfloat16)
            arrived[way] = along(value, way, senders)
    total = parts[-1].astype(jnp.float32)
    total = total + arrived[1].astype(jnp.float32) + arrived[-1].astype(jnp.float32)
    return total.astype(jnp.bfloat16)


def shards(hidden, start, w_query, w_key_value, w_out, cache):
    gx_count, gy_count = lax.axis_size("gx"), lax.axis_size("gy")
    fits = (
        gx_count == 4
        and gy_count == 8
        and w_query.shape[1] == 4 * HD
        and w_key_value.shape[2] == 2 * HD
        and 2 * hidden.shape[0] == WINDOW
    )
    run = line_shards if fits else plain_shards
    return run(hidden, start, w_query, w_key_value, w_out, cache)


def solution(mesh):
    return jax.shard_map(
        shards,
        mesh=mesh,
        in_specs=(
            P("gy", "gx"),
            P(),
            P("gx", "gy"),
            P("gx", None, "gy"),
            P("gy", "gx"),
            P(None, None, "gy"),
        ),
        out_specs=P("gy", "gx"),
        check_vma=False,
    )
```
